128 devices in a mesh: seq: 64 (over z, y, x), head: 2 (over core).
Axes of the slice: x: 4, y: 4, z: 4, core: 2. Of those that a mesh axis runs over, the one named last changes fastest.
Arguments:
- query_states: bfloat16 [32768, 2048], P('seq', 'head'), may hold values from -4.8125 to 4.8125
- key_states: bfloat16 [32768, 2048], P('seq', 'head'), may hold values from -4.8125 to 4.8125
- value_states: bfloat16 [32768, 2048], P('seq', 'head'), may hold values from -6 to 6
- doc_ids: int32 [64], P('seq'), may hold values from 0 to 15, as said below
- pair_table: int32 [192, 2], P('seq'), may hold values from 0 to 63, as said below
- out_weight: bfloat16 [2048, 4096], P('head'), may hold values from -1 to 1
Outputs:
- projected: bfloat16 [32768, 4096], P(('seq', 'head'))
The draws below stay inside these ranges and needn't reach their ends.
Inputs may be any that keep to these rules, and one draw needn't show every extreme that they name: `doc_ids`: consecutive from 0 and non-decreasing along the blocks. Every document covers 2 to 8 blocks and lies inside one aligned group of 16 blocks; each group holds four documents: one of 8 blocks, and at least one of 2. `pair_table`: each row holds two blocks a < b of one aligned group of 16 blocks; no row appears twice. In each aligned group exactly 24 rows pair two distinct blocks of one document; which of a document's block pairs are listed is arbitrary, and the others are not listed. The 3 rows of one index of seq hold 1 or 2 same-document rows, in no fixed order; its other rows pair blocks of different documents.
All inputs are finite; a program needn't handle non-finite values.
Results may differ from the reference program's by a relative error of at most 0.0053.
Values may be sent and summed in bfloat16 or wider, within the bound.
A program may use at most 192 MiB of HBM per device.

```python
import jax
import jax.numpy as jnp
import numpy as np
from jax import lax

D = 4096
HD = 128
H = 16
BLK = 512
BLOCKS = 64
TOKENS = 32768
GROUP = 16
DOC_MOST = 8
P_DEV = 3
LISTED = 24


def arrangements(pieces):
    if len(pieces) == 1:
        return [list(pieces)]
    results = []
    for position in range(len(pieces)):
        if pieces[position] in pieces[:position]:
            continue
        remain = pieces[:position] + pieces[position + 1:]
        for ending in arrangements(remain):
            results.append([pieces[position]] + ending)
    return results


def group_layouts():
    labels_all = []
    for multiset in ([8, 4, 2, 2], [8, 3, 3, 2]):
        for order_now in arrangements(multiset):
            labels_now = []
            for number, length_now in enumerate(order_now):
                labels_now.extend([number] * length_now)
            labels_all.append(labels_now)
    layout_table = np.array(labels_all, dtype=np.int32)
    return (layout_table, layout_table.max(axis=1) + 1)


def block_labels(key):
    layout_table, doc_counts = group_layouts()
    groups = BLOCKS // GROUP
    picked = jax.random.randint(key, (groups,), 0, layout_table.shape[0])
    labels_now = jnp.asarray(layout_table)[picked]
    counts_now = jnp.asarray(doc_counts)[picked]
    offsets = jnp.cumsum(counts_now) - counts_now
    return labels_now + offsets[:, None]


def draw_doc_ids(key, part):
    labels_now = block_labels(key)
    return labels_now.reshape(-1).astype(jnp.int32)


def draw_pair_table(key, part):
    labels_now = block_labels(key)
    own_key = jax.random.fold_in(key, 5)
    order_key, slot_key, listed_key, device_key = jax.random.split(own_key, 4)
    groups = BLOCKS // GROUP
    lower_np, upper_np = np.triu_indices(GROUP, 1)
    within = int(lower_np.shape[0])
    shared_grid = labels_now[:, lower_np] == labels_now[:, upper_np]
    spread = 1 << 20
    local_scores = jax.random.randint(listed_key, (groups, within), 0, spread) * within + jnp.arange(within, dtype=jnp.int32)[None, :]
    local_order = jnp.where(shared_grid, local_scores, local_scores + spread * within)
    local_rank = jnp.argsort(jnp.argsort(local_order, axis=1), axis=1)
    listed_now = (shared_grid & (local_rank < LISTED)).reshape(-1)
    shared = shared_grid.reshape(-1)
    base_np = (np.arange(groups) * GROUP)[:, None]
    lower_block = jnp.asarray((base_np + lower_np[None, :]).reshape(-1).astype(np.int32))
    upper_block = jnp.asarray((base_np + upper_np[None, :]).reshape(-1).astype(np.int32))
    total_pairs = lower_block.shape[0]
    random_ranks = jax.random.permutation(order_key, total_pairs)
    sort_key = jnp.where(listed_now, random_ranks, jnp.where(shared, random_ranks + 2 * total_pairs, random_ranks + total_pairs))
    chosen = jnp.argsort(sort_key)[:P_DEV * BLOCKS]
    dealt_rows = chosen.reshape(P_DEV, BLOCKS).T
    dealt_rows = dealt_rows[jax.random.permutation(device_key, BLOCKS)]
    shuffle_scores = jax.random.randint(slot_key, (BLOCKS, P_DEV), 0, 1024) * P_DEV + jnp.arange(P_DEV)
    dealt_rows = jnp.take_along_axis(dealt_rows, jnp.argsort(shuffle_scores, axis=1), axis=1).reshape(-1)
    return jnp.stack([lower_block[dealt_rows], upper_block[dealt_rows]], axis=1).astype(jnp.int32)


def draw_query_states(key, part):
    own_key = jax.random.fold_in(key, 11)
    return jnp.clip(1.4 * jax.random.normal(own_key, (TOKENS, H * HD), jnp.float32), -4.8, 4.8).astype(jnp.bfloat16)


def draw_key_states(key, part):
    own_key = jax.random.fold_in(key, 12)
    return jnp.clip(1.4 * jax.random.normal(own_key, (TOKENS, H * HD), jnp.float32), -4.8, 4.8).astype(jnp.bfloat16)


def level_of(rng, extent, cuts, least, largest):
    loudness = 1.0
    for axis_at, parts in cuts:
        draws = jax.random.uniform(jax.random.fold_in(jax.random.fold_in(rng, 6), axis_at), (parts,), jnp.float32, least / len(cuts), largest / len(cuts))
        loudness = loudness * jnp.repeat(jnp.exp(draws), extent[axis_at] // parts).reshape((-1,) + (1,) * (len(extent) - 1 - axis_at))
    return loudness


def noise(stream_key, dims, width, reach, shards=(), held_as=jnp.bfloat16):
    values = jax.random.normal(stream_key, dims, jnp.float32) * width
    if len(shards) > 0:
        values = level_of(stream_key, dims, shards, -0.22, 0.18) * values
    return jnp.clip(values, min=-reach, max=reach).astype(held_as)


def setup_inputs(seed: int = 0) -> dict:
    key_list = jax.random.split(jax.random.key(seed), 7)
    return {
        "query_states": draw_query_states(jax.random.fold_in(key_list[6], 71), 0),
        "key_states": draw_key_states(jax.random.fold_in(key_list[6], 71), 0),
        "value_states": noise(key_list[2], (TOKENS, H * HD), 1.0, 6.0, ((0, 64), (1, 2))),
        "doc_ids": draw_doc_ids(jax.random.fold_in(key_list[6], 71), 0),
        "pair_table": draw_pair_table(jax.random.fold_in(key_list[6], 71), 0),
        "out_weight": noise(key_list[5], (H * HD, D), (H * HD * 8 // BLK) ** -0.5, 1.0, ((0, 2),)),
    }


def reference(query_states, key_states, value_states, doc_ids, pair_table, out_weight):
    blocks = doc_ids.shape[0]
    columns = query_states.shape[1]
    head_count = columns // HD
    block_rows = query_states.shape[0] // blocks
    listed = jnp.zeros((blocks, blocks), jnp.int32).at[pair_table[:, 0], pair_table[:, 1]].set(1)
    listed = (listed + listed.T) > 0
    same_doc = doc_ids[:, None] == doc_ids[None, :]
    indices = jnp.arange(blocks, dtype=jnp.int32)
    attends = (indices[:, None] == indices[None, :]) | (listed & same_doc)
    earlier = jnp.sum((same_doc & (indices[None, :] < indices[:, None])).astype(jnp.int32), axis=1).astype(jnp.int32)
    starts = (indices - earlier).astype(jnp.int32)
    query_blocks = query_states.reshape(blocks, block_rows, head_count, HD)
    padding = jnp.zeros((DOC_MOST, block_rows, head_count, HD), key_states.dtype)
    key_blocks = jnp.concatenate([key_states.reshape(blocks, block_rows, head_count, HD), padding], 0)
    value_blocks = jnp.concatenate([value_states.reshape(blocks, block_rows, head_count, HD), padding], 0)
    attends_padded = jnp.concatenate([attends, jnp.zeros((blocks, DOC_MOST), dtype=bool)], 1)
    score_scale = HD ** -0.5

    def one_block(which_block):
        key_span = (starts[which_block] + jnp.arange(DOC_MOST, dtype=jnp.int32)).astype(jnp.int32)
        alive_tiles = attends_padded[which_block, key_span]
        key_tiles = key_blocks[key_span].astype(jnp.float32)
        value_tiles = value_blocks[key_span].astype(jnp.float32)
        query_rows = query_blocks[which_block].astype(jnp.float32)

        def visit_tile(running, tile):
            row_max, totals, mixed_sum = running
            key_rows, value_rows, alive_tile = tile
            scores = jnp.einsum("qhd,khd->hqk", query_rows, key_rows) * score_scale
            new_max = jnp.maximum(row_max, jnp.max(scores, axis=-1))
            shrink = jnp.exp(row_max - new_max)
            weights = jnp.exp(scores - new_max[:, :, None])
            new_totals = shrink * totals + jnp.sum(weights, axis=-1)
            rounded = lax.optimization_barrier(weights.astype(jnp.bfloat16))
            product = jnp.einsum("hqk,khd->qhd", rounded.astype(jnp.float32), value_rows)
            new_mixed = shrink.T[:, :, None] * mixed_sum + product
            return (jnp.where(alive_tile, new_max, row_max), jnp.where(alive_tile, new_totals, totals), jnp.where(alive_tile, new_mixed, mixed_sum)), None

        start_state = (jnp.full((head_count, block_rows), -jnp.inf, jnp.float32), jnp.zeros((head_count, block_rows), jnp.float32), jnp.zeros((block_rows, head_count, HD), jnp.float32))
        final_state, unused = lax.scan(visit_tile, start_state, (key_tiles, value_tiles, alive_tiles))
        row_max, totals, mixed_sum = final_state
        attended = (mixed_sum / totals.T[:, :, None]).astype(jnp.bfloat16).reshape(block_rows, columns)
        return jnp.dot(attended, out_weight, preferred_element_type=jnp.float32).astype(jnp.bfloat16)

    result = lax.map(one_block, indices)
    return result.reshape(blocks * block_rows, out_weight.shape[1])
```

```python
import functools

import jax
import jax.numpy as jnp
from jax import lax
from jax.experimental import pallas as pl
from jax.experimental.pallas import tpu as pltpu
from jax.sharding import PartitionSpec as P

HD = 128
BLK = 512
GROUP = 16
SIDE = 4
HALF = BLK // 2
TILES = 64
CHUNKS = 2
ROWS = HALF // CHUNKS
COLS = 512
LOG2E = 1.4426950408889634
MESH = pl.DeviceIdType.MESH

K, V, KF, VF, Q, O = 0, 1, 2, 3, 4, 4 + CHUNKS
KINDS = 4 + 2 * CHUNKS


def kernel(
    q_in, k_in, v_in, doc_in, pair_in, w_in, out,
    kbuf, vbuf, state, wbuf, meta, list_v, list_s, stage, *rest,
):
    qbuf, obuf, att = rest[:CHUNKS], rest[CHUNKS : 2 * CHUNKS], rest[2 * CHUNKS : 3 * CHUNKS]
    send_sem, recv_sem, meta_send, meta_recv, far_send, far_recv, w_sem, out_sem, list_sem = rest[3 * CHUNKS :]
    s, c = lax.axis_index("seq"), lax.axis_index("head")
    plane = s // GROUP
    base = plane * GROUP
    p = s - base

    def remote(src, dst, ssem, rsem, seq, core):
        return pltpu.make_async_remote_copy(
            src_ref=src, dst_ref=dst, send_sem=ssem, recv_sem=rsem,
            device_id=(seq, core), device_id_type=MESH,
        )

    def arrived(ref, sem):
        pltpu.make_async_copy(ref, ref, sem).wait()

    barrier = pltpu.get_barrier_semaphore()

    def greet(n, carry):
        pl.semaphore_signal(barrier, inc=1, device_id=(base + (p + n) % GROUP, c), device_id_type=MESH)
        return carry

    def greet_other(n, carry):
        pl.semaphore_signal(barrier, inc=1, device_id=(base + (p + n) % GROUP, 1 - c), device_id_type=MESH)
        return carry

    def greet_far(n, carry):
        pl.semaphore_signal(barrier, inc=1, device_id=((plane + n) % 4 * GROUP + p, c), device_id_type=MESH)
        return carry

    lax.fori_loop(1, GROUP, greet, 0)
    lax.fori_loop(0, GROUP, greet_other, 0)
    lax.fori_loop(1, 4, greet_far, 0)
    lane = lax.broadcasted_iota(jnp.int32, (8, 128), 1)
    row = jnp.where(lane == 0, doc_in[0], 0)
    for r in range(3):
        row = jnp.where(lane == r + 1, pair_in[r, 0] * 64 + pair_in[r, 1], row)
    meta[pl.ds(s, 1)] = row[None]
    pl.semaphore_wait(barrier, 2 * GROUP - 1 + 3)

    def meta_copy(n):
        return remote(
            meta.at[pl.ds(s, 1)], meta.at[pl.ds(s, 1)], meta_send.at[n], meta_recv.at[p],
            base + (p + n) % GROUP, c,
        )

    def far_copy(n):
        rows = pl.ds(base, GROUP)
        return remote(meta.at[rows], meta.at[rows], far_send.at[n], far_recv.at[plane], (plane + n) % 4 * GROUP + p, c)

    lax.fori_loop(1, GROUP, lambda n, x: (meta_copy(n).start(), x)[1], 0)

    def deal(kind, ref, dst, first_row, rows, start):
        def step(n, carry):
            i, j = (n // 2 + p) % 8, n % 2
            seq = base + 8 * c + i
            mine = (seq == s) & (j == c)
            src = ref.at[pl.ds(pl.multiple_of(j * HALF + first_row, 128), rows), pl.ds(pl.multiple_of(i * HD, HD), HD)]
            to = dst(j)

            @pl.when(mine)
            def _():
                if start:
                    pltpu.make_async_copy(src, to, recv_sem.at[kind, p]).start()

            @pl.when(jnp.logical_not(mine))
            def _():
                copy = remote(src, to, send_sem.at[kind, n], recv_sem.at[kind, p], seq, j)
                if start:
                    copy.start()
                else:
                    copy.wait_send()

            return carry

        lax.fori_loop(0, GROUP, step, 0)

    def half_of(buf, b, j):
        return buf.at[b, pl.ds(pl.multiple_of(j * HALF, HALF), HALF)]

    def deal_k(start):
        deal(K, k_in, lambda j: half_of(kbuf, p, j), 0, HALF, start)

    def deal_v(start):
        deal(V, v_in, lambda j: half_of(vbuf, p, j), 0, HALF, start)

    def deal_q(u, start):
        deal(Q + u, q_in, lambda j: qbuf[u].at[p], u * ROWS, ROWS, start)

    deal_k(True)
    deal_v(True)
    for u in range(CHUNKS):
        deal_q(u, True)

    w_rows = pl.ds(pl.multiple_of(c * 1024, 1024), 1024)
    w_other = pl.ds(pl.multiple_of((1 - c) * 1024, 1024), 1024)
    w_own = pltpu.make_async_copy(w_in, wbuf.at[w_rows], w_sem.at[0])
    w_sent = remote(w_in, wbuf.at[w_rows], w_sem.at[1], w_sem.at[2], s, 1 - c)
    w_own.start()
    w_sent.start()

    lax.fori_loop(1, GROUP, lambda n, x: (arrived(meta.at[pl.ds(base + (p + n) % GROUP, 1)], meta_recv.at[(p + n) % GROUP]), x)[1], 0)
    lax.fori_loop(1, 4, lambda n, x: (far_copy(n).start(), x)[1], 0)
    lax.fori_loop(
        1, 4,
        lambda n, x: (arrived(meta.at[pl.ds((plane + n) % 4 * GROUP, GROUP)], far_recv.at[(plane + n) % 4]), x)[1],
        0,
    )

    table = meta[:, 0, :]
    cell = lax.broadcasted_iota(jnp.int32, (64, 256), 1)
    place = lax.broadcasted_iota(jnp.int32, (64, 256), 0)
    qa, ka = cell // GROUP + base, cell % GROUP + base
    code = jnp.minimum(qa, ka) * 64 + jnp.maximum(qa, ka)
    hit = (code == table[:, 1:2]) | (code == table[:, 2:3]) | (code == table[:, 3:4])
    listed = jnp.max(jnp.where(hit, 1.0, 0.0), axis=0, keepdims=True)
    docs = table[:, 0:1]
    doc_q = jnp.sum(jnp.where(place == qa, docs, 0).astype(jnp.float32), axis=0, keepdims=True)
    doc_k = jnp.sum(jnp.where(place == ka, docs, 0).astype(jnp.float32), axis=0, keepdims=True)
    alive = jnp.where((qa[:1] == ka[:1]) | ((listed > 0.5) & (doc_q == doc_k)), 1.0, 0.0)
    upto = jnp.where(
        lax.broadcasted_iota(jnp.int32, (256, 256), 0) <= lax.broadcasted_iota(jnp.int32, (256, 256), 1), 1.0, 0.0
    )
    rank = jnp.dot(
        jnp.broadcast_to(alive, (16, 256)).astype(jnp.bfloat16), upto.astype(jnp.bfloat16),
        preferred_element_type=jnp.float32,
    )[:1]
    pick = jnp.where((alive > 0.5) & (rank == (place + 1).astype(jnp.float32)), 1.0, 0.0)
    cells = jnp.sum(pick * cell.astype(jnp.float32), axis=1, keepdims=True)
    rank_64 = jnp.broadcast_to(rank, (64, 256))
    ends = jnp.sum(jnp.where(cell == place * GROUP + GROUP - 1, rank_64 - 1.0, 0.0), axis=1, keepdims=True)
    opens = jnp.max(
        jnp.where((cell % GROUP == GROUP - 1) & (rank_64 == place.astype(jnp.float32)), 1.0, 0.0), axis=1, keepdims=True
    )
    wide = lax.broadcasted_iota(jnp.int32, (64, 128), 1)
    table_out = jnp.where(wide == 0, cells, jnp.where(wide == 1, opens, jnp.where(wide == 2, ends, 0.0)))
    list_v[...] = table_out.astype(jnp.int32)
    to_scalar = pltpu.make_async_copy(list_v, list_s, list_sem)
    to_scalar.start()
    to_scalar.wait()

    def forward(kind, buf, b):
        return remote(half_of(buf, b, c), half_of(buf, b, c), send_sem.at[kind + 2, b], recv_sem.at[kind + 2, b], s, 1 - c)

    for kind, buf in ((K, kbuf), (V, vbuf)):

        def pass_on(n, carry, kind=kind, buf=buf):
            b = (p + n) % GROUP
            arrived(half_of(buf, b, c), recv_sem.at[kind, b])
            forward(kind, buf, b).start()
            return carry

        lax.fori_loop(0, GROUP, pass_on, 0)

    for kind, buf in ((K, kbuf), (V, vbuf)):

        def landed(b, carry, kind=kind, buf=buf):
            arrived(half_of(buf, b, 1 - c), recv_sem.at[kind + 2, b])
            return carry

        lax.fori_loop(0, GROUP, landed, 0)

    scale = jnp.float32(HD**-0.5 * LOG2E)
    ones = jnp.ones((BLK, HD), jnp.bfloat16)

    def give_back(u, n):
        to = (p + n) % GROUP
        dst = att[u].at[:, pl.ds(pl.multiple_of(p * HD, HD), HD)]
        return remote(obuf[u].at[to], dst, send_sem.at[O + u, n], recv_sem.at[O + u, p], base + to, c)

    def attend(u):
        lax.fori_loop(0, GROUP, lambda b, x: (arrived(qbuf[u].at[b], recv_sem.at[Q + u, b]), x)[1], 0)

        def visit(t, carry):
            top, total = carry
            at = jnp.clip(list_s[t, 0], 0, GROUP * GROUP - 1)
            opened = list_s[t, 1] == 1
            key = at % GROUP
            scores = lax.dot_general(
                qbuf[u][at // GROUP], kbuf[key], (((1,), (1,)), ((), ())), preferred_element_type=jnp.float32
            )
            top = jnp.where(opened, -jnp.inf, top)
            new_top = jnp.maximum(top, jnp.max(scores, axis=1, keepdims=True))
            weights = jnp.exp2((scores - new_top) * scale).astype(jnp.bfloat16)
            shrink = jnp.exp2((top - new_top) * scale)
            values = jnp.concatenate([vbuf[key], ones], axis=1)
            total = shrink * total + jnp.dot(weights, values, preferred_element_type=jnp.float32)
            state[t] = total
            return new_top, total

        start = (jnp.full((ROWS, 1), -jnp.inf, jnp.float32), jnp.zeros((ROWS, 2 * HD), jnp.float32))
        lax.fori_loop(0, TILES, visit, start, unroll=4)

        def finish(b, carry):
            total = state[jnp.clip(list_s[b, 2], 0, TILES - 1)]
            obuf[u][b] = (total[:, :HD] / total[:, HD:]).astype(jnp.bfloat16)
            return carry

        lax.fori_loop(0, GROUP, finish, 0)
        lax.fori_loop(1, GROUP, lambda n, x: (give_back(u, n).start(), x)[1], 0)
        pltpu.make_async_copy(
            obuf[u].at[p], att[u].at[:, pl.ds(pl.multiple_of(p * HD, HD), HD)], recv_sem.at[O + u, p]
        ).start()

    def out_copy(u):
        return pltpu.make_async_copy(stage.at[u], out.at[pl.ds(u * ROWS, ROWS)], out_sem.at[u])

    def project(u):
        lax.fori_loop(
            0, GROUP,
            lambda h, x: (arrived(att[u].at[:, pl.ds(pl.multiple_of(h * HD, HD), HD)], recv_sem.at[O + u, h]), x)[1],
            0,
        )

        def tile(n, carry):
            cols = pl.ds(pl.multiple_of(n * COLS, COLS), COLS)
            stage[u, :, cols] = jnp.dot(att[u][...], wbuf[:, cols], preferred_element_type=jnp.float32).astype(jnp.bfloat16)
            return carry

        lax.fori_loop(0, wbuf.shape[1] // COLS, tile, 0)
        out_copy(u).start()

    for u in range(CHUNKS):
        attend(u)
    w_own.wait()
    w_sent.wait_recv()
    for u in range(CHUNKS):
        project(u)

    lax.fori_loop(1, GROUP, lambda n, x: (meta_copy(n).wait_send(), x)[1], 0)
    lax.fori_loop(1, 4, lambda n, x: (far_copy(n).wait_send(), x)[1], 0)
    deal_k(False)
    deal_v(False)
    for u in range(CHUNKS):
        deal_q(u, False)
        lax.fori_loop(1, GROUP, lambda n, x, u=u: (give_back(u, n).wait_send(), x)[1], 0)
    lax.fori_loop(0, GROUP, lambda b, x: (forward(K, kbuf, b).wait_send(), x)[1], 0)
    lax.fori_loop(0, GROUP, lambda b, x: (forward(V, vbuf, b).wait_send(), x)[1], 0)
    w_sent.wait_send()
    for u in range(CHUNKS):
        out_copy(u).wait()


def local(query_states, key_states, value_states, doc_ids, pair_table, out_weight):
    bf16, dma = jnp.bfloat16, pltpu.SemaphoreType.DMA
    anywhere, scalars = pl.BlockSpec(memory_space=pl.ANY), pl.BlockSpec(memory_space=pltpu.SMEM)
    width = out_weight.shape[1]
    return pl.pallas_call(
        kernel,
        out_shape=jax.ShapeDtypeStruct((HALF, width), bf16),
        in_specs=[anywhere, anywhere, anywhere, scalars, scalars, anywhere],
        out_specs=anywhere,
        scratch_shapes=[
            pltpu.VMEM((GROUP, BLK, HD), bf16),
            pltpu.VMEM((GROUP, BLK, HD), bf16),
            pltpu.VMEM((TILES, ROWS, 2 * HD), jnp.float32),
            pltpu.VMEM((2048, width), bf16),
            pltpu.VMEM((64, 8, 128), jnp.int32),
            pltpu.VMEM((64, 128), jnp.int32),
            pltpu.SMEM((64, 128), jnp.int32),
            pltpu.VMEM((CHUNKS, ROWS, width), bf16),
        ]
        + [pltpu.VMEM((GROUP, ROWS, HD), bf16)] * CHUNKS
        + [pltpu.VMEM((GROUP, ROWS, HD), bf16)] * CHUNKS
        + [pltpu.VMEM((ROWS, 2048), bf16)] * CHUNKS
        + [dma((KINDS, GROUP)), dma((KINDS, GROUP)), dma((GROUP,)), dma((GROUP,)), dma((4,)), dma((4,)),
           dma((3,)), dma((CHUNKS,)), dma],
        compiler_params=pltpu.CompilerParams(
            collective_id=0, has_side_effects=True, vmem_limit_bytes=56 << 20
        ),
    )(query_states, key_states, value_states, doc_ids, pair_table, out_weight)


def solution(mesh):
    placed = (
        P("seq", "head"),
        P("seq", "head"),
        P("seq", "head"),
        P("seq"),
        P("seq", None),
        P("head", None),
    )
    return jax.shard_map(
        local, mesh=mesh, in_specs=placed, out_specs=P(("seq", "head"), None), check_vma=False
    )
```

```python
import jax
import jax.numpy as jnp
from jax import lax
from jax.experimental import pallas as pl
from jax.experimental.pallas import tpu as pltpu
from jax.sharding import PartitionSpec as P

HD = 128
BLK = 512
GROUP = 16
HALF = BLK // 2
TILES = 64
CHUNKS = 2
ROWS = HALF // CHUNKS
COLS = 512
LOG2E = 1.4426950408889634
MESH = pl.DeviceIdType.MESH

K, V, KF, VF, Q, O = 0, 1, 2, 3, 4, 4 + CHUNKS
KINDS = 4 + 2 * CHUNKS
GATE = False
UNROLL = 16


def kernel(
    q_in, k_in, v_in, doc_in, pair_in, w_in, out,
    kbuf, vbuf, state, wbuf, meta, list_v, list_s, doc_s, pair_s, stage, *rest,
):
    qbuf, obuf, att = rest[:CHUNKS], rest[CHUNKS : 2 * CHUNKS], rest[2 * CHUNKS : 3 * CHUNKS]
    send_sem, recv_sem, block_sem, meta_sem, w_sem, out_sem, own_sem = rest[3 * CHUNKS :]
    s, c = lax.axis_index("seq"), lax.axis_index("head")
    plane = s // GROUP
    base = plane * GROUP
    p = s - base

    def remote(src, dst, ssem, rsem, seq, core):
        return pltpu.make_async_remote_copy(
            src_ref=src, dst_ref=dst, send_sem=ssem, recv_sem=rsem,
            device_id=(seq, core), device_id_type=MESH,
        )

    def arrived(ref, sem):
        pltpu.make_async_copy(ref, ref, sem).wait()

    barrier = pltpu.get_barrier_semaphore()

    def greet(n, carry):
        pl.semaphore_signal(barrier, inc=1, device_id=(base + (p + n) % GROUP, c), device_id_type=MESH)
        pl.semaphore_signal(barrier, inc=1, device_id=(base + (p + n) % GROUP, 1 - c), device_id_type=MESH)
        return carry

    def greet_far(n, carry):
        pl.semaphore_signal(barrier, inc=1, device_id=((plane + n) % 4 * GROUP + p, c), device_id_type=MESH)
        return carry

    lax.fori_loop(1, GROUP, greet, 0)
    lax.fori_loop(1, 4, greet_far, 0)
    pl.semaphore_signal(barrier, inc=1, device_id=(s, 1 - c), device_id_type=MESH)

    w_rows = pl.ds(pl.multiple_of(c * 1024, 1024), 1024)
    w_own = pltpu.make_async_copy(w_in, wbuf.at[w_rows], w_sem.at[0])
    w_own.start()
    doc_copy = pltpu.make_async_copy(doc_in, doc_s, own_sem.at[0])
    pair_copy = pltpu.make_async_copy(pair_in, pair_s, own_sem.at[1])
    doc_copy.start()
    pair_copy.start()
    doc_copy.wait()
    pair_copy.wait()
    lane = lax.broadcasted_iota(jnp.int32, (8, 128), 1)
    row = jnp.where(lane == 0, doc_s[0], 0)
    for r in range(3):
        row = jnp.where(lane == r + 1, pair_s[r, 0] * 64 + pair_s[r, 1], row)
    meta[pl.ds(s, 1)] = row[None]
    pl.semaphore_wait(barrier, 2 * GROUP - 1 + 3)

    def meta_copy(n, carry):
        own = meta.at[pl.ds(s, 1)]
        remote(own, own, meta_sem.at[0], meta_sem.at[1], base + (p + n) % GROUP, c).start()
        return carry

    def far_copy(n, carry):
        rows = meta.at[pl.ds(base, GROUP)]
        remote(rows, rows, meta_sem.at[2], meta_sem.at[3], (plane + n) % 4 * GROUP + p, c).start()
        return carry

    lax.fori_loop(1, GROUP, meta_copy, 0)

    def deal(kind, ref, dst, recv, first_row, rows):
        def step(n, carry):
            i = (n + p) % 8
            seq = base + 8 * c + i
            for j in range(2):
                src = ref.at[pl.ds(j * HALF + first_row, rows), pl.ds(pl.multiple_of(i * HD, HD), HD)]
                mine = (seq == s) & (c == j)

                @pl.when(mine)
                def _(src=src, j=j):
                    pltpu.make_async_copy(src, dst(j), recv).start()

                @pl.when(jnp.logical_not(mine))
                def _(src=src, j=j):
                    remote(src, dst(j), send_sem.at[kind], recv, seq, j).start()

            return carry

        lax.fori_loop(0, 8, step, 0)

    def dealt(kind, rows):
        own = p // 8 == c

        @pl.when(own)
        def _():
            arrived(kbuf.at[pl.ds(0, GROUP - 1), pl.ds(0, rows)], send_sem.at[kind])

        @pl.when(jnp.logical_not(own))
        def _():
            arrived(kbuf.at[:, pl.ds(0, rows)], send_sem.at[kind])

    def half_of(buf, b, j):
        return buf.at[b, pl.ds(pl.multiple_of(j * HALF, HALF), HALF)]

    def deal_q(u):
        deal(Q + u, q_in, lambda j: qbuf[u].at[p], recv_sem.at[Q + u], u * ROWS, ROWS)

    deal(K, k_in, lambda j: half_of(kbuf, p, j), block_sem.at[K, p], 0, HALF)
    deal(V, v_in, lambda j: half_of(vbuf, p, j), block_sem.at[V, p], 0, HALF)
    w_sent = remote(w_in, wbuf.at[w_rows], w_sem.at[1], w_sem.at[2], s, 1 - c)
    w_sent.start()
    if not GATE:
        for u in range(CHUNKS):
            deal_q(u)

    arrived(meta.at[pl.ds(0, GROUP - 1)], meta_sem.at[1])
    lax.fori_loop(1, 4, far_copy, 0)
    arrived(meta.at[pl.ds(0, 3 * GROUP)], meta_sem.at[3])

    table = meta[:, 0, :]
    cell = lax.broadcasted_iota(jnp.int32, (64, 256), 1)
    place = lax.broadcasted_iota(jnp.int32, (64, 256), 0)
    qa, ka = cell // GROUP + base, cell % GROUP + base
    code = jnp.minimum(qa, ka) * 64 + jnp.maximum(qa, ka)
    hit = (code == table[:, 1:2]) | (code == table[:, 2:3]) | (code == table[:, 3:4])
    listed = jnp.max(jnp.where(hit, 1.0, 0.0), axis=0, keepdims=True)
    docs = table[:, 0:1]
    doc_q = jnp.sum(jnp.where(place == qa, docs, 0).astype(jnp.float32), axis=0, keepdims=True)
    doc_k = jnp.sum(jnp.where(place == ka, docs, 0).astype(jnp.float32), axis=0, keepdims=True)
    alive = jnp.where((qa[:1] == ka[:1]) | ((listed > 0.5) & (doc_q == doc_k)), 1.0, 0.0)
    upto = jnp.where(
        lax.broadcasted_iota(jnp.int32, (256, 256), 0) <= lax.broadcasted_iota(jnp.int32, (256, 256), 1), 1.0, 0.0
    )
    rank = jnp.dot(
        jnp.broadcast_to(alive, (16, 256)).astype(jnp.bfloat16), upto.astype(jnp.bfloat16),
        preferred_element_type=jnp.float32,
    )[:1]
    pick = jnp.where((alive > 0.5) & (rank == (place + 1).astype(jnp.float32)), 1.0, 0.0)
    cells = jnp.sum(pick * cell.astype(jnp.float32), axis=1, keepdims=True)
    rank_64 = jnp.broadcast_to(rank, (64, 256))
    ends = jnp.sum(jnp.where(cell == place * GROUP + GROUP - 1, rank_64 - 1.0, 0.0), axis=1, keepdims=True)
    opens = jnp.max(
        jnp.where((cell % GROUP == GROUP - 1) & (rank_64 == place.astype(jnp.float32)), 1.0, 0.0), axis=1, keepdims=True
    )
    wide = lax.broadcasted_iota(jnp.int32, (64, 128), 1)
    table_out = jnp.where(wide == 0, cells, jnp.where(wide == 1, opens, jnp.where(wide == 2, ends, 0.0)))
    list_v[...] = table_out.astype(jnp.int32)
    to_scalar = pltpu.make_async_copy(list_v, list_s, own_sem.at[0])
    to_scalar.start()
    to_scalar.wait()

    def pass_all(kind, buf):
        def pass_on(n, carry):
            b = (p + n) % GROUP
            part = half_of(buf, b, c)
            arrived(part, block_sem.at[kind, b])
            remote(part, part, send_sem.at[kind + 2], recv_sem.at[kind + 2], s, 1 - c).start()
            return carry

        lax.fori_loop(0, GROUP, pass_on, 0)

    pass_all(K, kbuf)
    if GATE:
        dealt(K, HALF)
        deal_q(0)
    pass_all(V, vbuf)
    if GATE:
        dealt(V, HALF)
        for u in range(1, CHUNKS):
            deal_q(u)
    other = pl.ds(pl.multiple_of((1 - c) * HALF, HALF), HALF)
    arrived(kbuf.at[:, other], recv_sem.at[KF])
    arrived(vbuf.at[:, other], recv_sem.at[VF])
    if not GATE:
        dealt(K, HALF)
        dealt(V, HALF)
    arrived(meta.at[pl.ds(0, GROUP - 1)], meta_sem.at[0])
    arrived(meta.at[pl.ds(0, 3 * GROUP)], meta_sem.at[2])
    arrived(kbuf.at[:, other], send_sem.at[KF])

    scale = jnp.float32(HD**-0.5 * LOG2E)
    ones = jnp.ones((BLK, HD), jnp.bfloat16)
    columns = pl.ds(pl.multiple_of(p * HD, HD), HD)

    def attend(u):
        arrived(qbuf[u], recv_sem.at[Q + u])

        def visit(t, carry):
            top, total = carry
            at = jnp.clip(list_s[t, 0], 0, GROUP * GROUP - 1)
            opened = list_s[t, 1] == 1
            key = at % GROUP
            scores = lax.dot_general(
                qbuf[u][at // GROUP], kbuf[key], (((1,), (1,)), ((), ())), preferred_element_type=jnp.float32
            )
            top = jnp.where(opened, -jnp.inf, top)
            new_top = jnp.maximum(top, jnp.max(scores, axis=1, keepdims=True))
            weights = jnp.exp2((scores - new_top) * scale).astype(jnp.bfloat16)
            shrink = jnp.exp2((top - new_top) * scale)
            values = jnp.concatenate([vbuf[key], ones], axis=1)
            total = shrink * total + jnp.dot(weights, values, preferred_element_type=jnp.float32)
            state[t] = total
            return new_top, total

        start = (jnp.full((ROWS, 1), -jnp.inf, jnp.float32), jnp.zeros((ROWS, 2 * HD), jnp.float32))
        lax.fori_loop(0, TILES, visit, start, unroll=UNROLL)

        def finish(n, carry):
            b = (p + n) % GROUP
            total = state[jnp.clip(list_s[b, 2], 0, TILES - 1)]
            obuf[u][b] = (total[:, :HD] / total[:, HD:]).astype(jnp.bfloat16)
            remote(obuf[u].at[b], att[u].at[:, columns], send_sem.at[O + u], recv_sem.at[O + u], base + b, c).start()
            return carry

        lax.fori_loop(1, GROUP, finish, 0)
        total = state[jnp.clip(list_s[p, 2], 0, TILES - 1)]
        obuf[u][p] = (total[:, :HD] / total[:, HD:]).astype(jnp.bfloat16)
        pltpu.make_async_copy(obuf[u].at[p], att[u].at[:, columns], recv_sem.at[O + u]).start()

    def out_copy(u):
        return pltpu.make_async_copy(stage.at[u], out.at[pl.ds(u * ROWS, ROWS)], out_sem.at[u])

    def project(u):
        arrived(att[u], recv_sem.at[O + u])

        def tile(n, carry):
            cols = pl.ds(pl.multiple_of(n * COLS, COLS), COLS)
            stage[u, :, cols] = jnp.dot(att[u][...], wbuf[:, cols], preferred_element_type=jnp.float32).astype(jnp.bfloat16)
            return carry

        lax.fori_loop(0, wbuf.shape[1] // COLS, tile, 0)
        out_copy(u).start()

    for u in range(CHUNKS):
        attend(u)
    w_own.wait()
    w_sent.wait()
    arrived(vbuf.at[:, other], send_sem.at[VF])
    for u in range(CHUNKS):
        dealt(Q + u, ROWS)
    for u in range(CHUNKS):
        project(u)
    for u in range(CHUNKS):
        arrived(obuf[u].at[pl.ds(0, GROUP - 1)], send_sem.at[O + u])
    for u in range(CHUNKS):
        out_copy(u).wait()


def local(query_states, key_states, value_states, doc_ids, pair_table, out_weight):
    bf16, dma = jnp.bfloat16, pltpu.SemaphoreType.DMA
    anywhere = pl.BlockSpec(memory_space=pl.ANY)
    width = out_weight.shape[1]
    return pl.pallas_call(
        kernel,
        out_shape=jax.ShapeDtypeStruct((HALF, width), bf16),
        in_specs=[anywhere] * 6,
        out_specs=anywhere,
        scratch_shapes=[
            pltpu.VMEM((GROUP, BLK, HD), bf16),
            pltpu.VMEM((GROUP, BLK, HD), bf16),
            pltpu.VMEM((TILES, ROWS, 2 * HD), jnp.float32),
            pltpu.VMEM((2048, width), bf16),
            pltpu.VMEM((64, 8, 128), jnp.int32),
            pltpu.VMEM((64, 128), jnp.int32),
            pltpu.SMEM((64, 128), jnp.int32),
            pltpu.SMEM((1,), jnp.int32),
            pltpu.SMEM((3, 2), jnp.int32),
            pltpu.VMEM((CHUNKS, ROWS, width), bf16),
        ]
        + [pltpu.VMEM((GROUP, ROWS, HD), bf16)] * CHUNKS
        + [pltpu.VMEM((GROUP, ROWS, HD), bf16)] * CHUNKS
        + [pltpu.VMEM((ROWS, 2048), bf16)] * CHUNKS
        + [dma((KINDS,)), dma((KINDS,)), dma((2, GROUP)), dma((4,)), dma((3,)), dma((CHUNKS,)), dma((2,))],
        compiler_params=pltpu.CompilerParams(
            collective_id=0, has_side_effects=True, vmem_limit_bytes=56 << 20
        ),
    )(query_states, key_states, value_states, doc_ids, pair_table, out_weight)


def solution(mesh):
    placed = (
        P("seq", "head"),
        P("seq", "head"),
        P("seq", "head"),
        P("seq"),
        P("seq", None),
        P("head", None),
    )
    return jax.shard_map(
        local, mesh=mesh, in_specs=placed, out_specs=P(("seq", "head"), None), check_vma=False
    )
```

```python
import functools

import jax
import jax.numpy as jnp
from jax import lax
from jax.experimental import pallas as pl
from jax.experimental.pallas import tpu as pltpu
from jax.sharding import PartitionSpec as P

HD = 128
BLK = 512
GROUP = 16
HALF = BLK // 2
TILES = 64
SIZES = (128, 128)
FIRSTS = (0, 128)
STEPS = ((0, 32, 0, 4), (32, 48, 4, 8), (48, 64, 8, 16))
PROJ_UNROLL = 4
STEP_X = sum(d << 2 * n for n, d in enumerate((2, 2, 1, 3, 1, 3, 0, 0)))
STEP_Y = sum(d << 2 * n for n, d in enumerate((1, 0, 1, 1, 0, 0, 1, 0)))
CHUNKS = len(SIZES)
MOST = max(SIZES)
COLS = 512
LOG2E = 1.4426950408889634
MESH = pl.DeviceIdType.MESH

K, V, KF, VF, Q, O = 0, 1, 2, 3, 4, 4 + CHUNKS
KINDS = 4 + 2 * CHUNKS


def kernel(
    q_in, k_in, v_in, doc_in, pair_in, w_in, out,
    kbuf, vbuf, state, wbuf, meta, list_v, list_s, doc_s, pair_s, *rest,
):
    qbuf, obuf = rest[:CHUNKS], rest[CHUNKS : 2 * CHUNKS]
    att, partial_sum, send_sem, recv_sem, back_sem, block_sem, meta_sem, w_sem, own_sem = rest[2 * CHUNKS :]
    s, c = lax.axis_index("seq"), lax.axis_index("head")
    plane = s // GROUP
    base = plane * GROUP
    p = s - base

    def remote(src, dst, ssem, rsem, seq, core):
        return pltpu.make_async_remote_copy(
            src_ref=src, dst_ref=dst, send_sem=ssem, recv_sem=rsem,
            device_id=(seq, core), device_id_type=MESH,
        )

    def arrived(ref, sem):
        pltpu.make_async_copy(ref, ref, sem).wait()

    x, y = p % 4, p // 4

    def block_at(place):
        step = place // 2 * 2
        return (y + (STEP_Y >> step & 3) + place % 2 * 2) % 4 * 4 + (x + (STEP_X >> step & 3)) % 4

    barrier = pltpu.get_barrier_semaphore()

    def greet(n, carry):
        pl.semaphore_signal(barrier, inc=1, device_id=(base + (p + n) % GROUP, c), device_id_type=MESH)
        pl.semaphore_signal(barrier, inc=1, device_id=(base + (p + n) % GROUP, 1 - c), device_id_type=MESH)
        return carry

    def greet_far(n, carry):
        pl.semaphore_signal(barrier, inc=1, device_id=((plane + n) % 4 * GROUP + p, c), device_id_type=MESH)
        return carry

    lax.fori_loop(1, GROUP, greet, 0)
    lax.fori_loop(1, 4, greet_far, 0)
    pl.semaphore_signal(barrier, inc=1, device_id=(s, 1 - c), device_id_type=MESH)

    w_rows = pl.ds(pl.multiple_of(c * 1024, 1024), 1024)
    w_own = pltpu.make_async_copy(w_in, wbuf.at[w_rows], w_sem.at[0])
    w_own.start()
    doc_copy = pltpu.make_async_copy(doc_in, doc_s, own_sem.at[0])
    pair_copy = pltpu.make_async_copy(pair_in, pair_s, own_sem.at[1])
    doc_copy.start()
    pair_copy.start()
    doc_copy.wait()
    pair_copy.wait()
    lane = lax.broadcasted_iota(jnp.int32, (8, 128), 1)
    row = jnp.where(lane == 0, doc_s[0], 0)
    for r in range(3):
        row = jnp.where(lane == r + 1, pair_s[0, r] * 64 + pair_s[1, r], row)
    meta[pl.ds(s, 1)] = row[None]
    pl.semaphore_wait(barrier, 2 * GROUP - 1 + 3)

    def meta_copy(n, carry):
        own = meta.at[pl.ds(s, 1)]
        remote(own, own, meta_sem.at[0], meta_sem.at[1], base + (p + n) % GROUP, c).start()
        return carry

    def far_copy(n, carry):
        rows = meta.at[pl.ds(base, GROUP)]
        remote(rows, rows, meta_sem.at[2], meta_sem.at[3], (plane + n) % 4 * GROUP + p, c).start()
        return carry

    lax.fori_loop(1, GROUP, meta_copy, 0)

    def deal(kind, ref, dst, recv, first_row, rows):
        def step(n, carry):
            i = (n + p) % 8
            seq = base + 8 * c + i
            for j in range(2):
                src = ref.at[pl.ds(j * HALF + first_row, rows), pl.ds(pl.multiple_of(i * HD, HD), HD)]
                mine = (seq == s) & (c == j)

                @pl.when(mine)
                def _(src=src, j=j):
                    pltpu.make_async_copy(src, dst(j), recv).start()

                @pl.when(jnp.logical_not(mine))
                def _(src=src, j=j):
                    remote(src, dst(j), send_sem.at[kind], recv, seq, j).start()

            return carry

        lax.fori_loop(0, 8, step, 0)

    def dealt(kind, rows):
        own = p // 8 == c

        @pl.when(own)
        def _():
            arrived(kbuf.at[pl.ds(0, GROUP - 1), pl.ds(0, rows)], send_sem.at[kind])

        @pl.when(jnp.logical_not(own))
        def _():
            arrived(kbuf.at[:, pl.ds(0, rows)], send_sem.at[kind])

    def half_of(buf, b, j):
        return buf.at[b, pl.ds(pl.multiple_of(j * HALF, HALF), HALF)]

    def deal_q(u):
        deal(Q + u, q_in, lambda j: qbuf[u].at[p], recv_sem.at[Q + u], FIRSTS[u], SIZES[u])

    deal(K, k_in, lambda j: half_of(kbuf, p, j), block_sem.at[K, p], 0, HALF)
    deal(V, v_in, lambda j: half_of(vbuf, p, j), block_sem.at[V, p], 0, HALF)
    w_sent = remote(w_in, wbuf.at[w_rows], w_sem.at[1], w_sem.at[2], s, 1 - c)
    w_sent.start()
    deal_q(0)

    arrived(meta.at[pl.ds(0, GROUP - 1)], meta_sem.at[1])
    lax.fori_loop(1, 4, far_copy, 0)
    arrived(meta.at[pl.ds(0, 3 * GROUP)], meta_sem.at[3])

    table = meta[:, 0, :]
    cell = lax.broadcasted_iota(jnp.int32, (64, 256), 1)
    place = lax.broadcasted_iota(jnp.int32, (64, 256), 0)
    qb = block_at(cell // GROUP)
    qa, ka = qb + base, cell % GROUP + base
    code = jnp.minimum(qa, ka) * 64 + jnp.maximum(qa, ka)
    hit = (code == table[:, 1:2]) | (code == table[:, 2:3]) | (code == table[:, 3:4])
    listed = jnp.max(jnp.where(hit, 1.0, 0.0), axis=0, keepdims=True)
    docs = table[:, 0:1]
    doc_q = jnp.sum(jnp.where(place == qa, docs, 0).astype(jnp.float32), axis=0, keepdims=True)
    doc_k = jnp.sum(jnp.where(place == ka, docs, 0).astype(jnp.float32), axis=0, keepdims=True)
    alive = jnp.where((qa[:1] == ka[:1]) | ((listed > 0.5) & (doc_q == doc_k)), 1.0, 0.0)
    upto = jnp.where(
        lax.broadcasted_iota(jnp.int32, (256, 256), 0) <= lax.broadcasted_iota(jnp.int32, (256, 256), 1), 1.0, 0.0
    )
    rank = jnp.dot(
        jnp.broadcast_to(alive, (16, 256)).astype(jnp.bfloat16), upto.astype(jnp.bfloat16),
        preferred_element_type=jnp.float32,
    )[:1]
    pick = jnp.where((alive > 0.5) & (rank == (place + 1).astype(jnp.float32)), 1.0, 0.0)
    cells = jnp.sum(pick * (qb * GROUP + cell % GROUP).astype(jnp.float32), axis=1, keepdims=True)
    rank_64 = jnp.broadcast_to(rank, (64, 256))
    ends = jnp.sum(jnp.where(cell == place * GROUP + GROUP - 1, rank_64 - 1.0, 0.0), axis=1, keepdims=True)
    opens = jnp.max(
        jnp.where((cell % GROUP == GROUP - 1) & (rank_64 == place.astype(jnp.float32)), 1.0, 0.0), axis=1, keepdims=True
    )
    wide = lax.broadcasted_iota(jnp.int32, (64, 128), 1)
    table_out = jnp.where(wide == 0, cells, jnp.where(wide == 1, opens, jnp.where(wide == 2, ends, 0.0)))
    list_v[...] = table_out.astype(jnp.int32)
    to_scalar = pltpu.make_async_copy(list_v, list_s, own_sem.at[0])
    to_scalar.start()
    to_scalar.wait()

    def pass_all(kind, buf):
        def pass_on(n, carry):
            b = (p + n) % GROUP
            part = half_of(buf, b, c)
            arrived(part, block_sem.at[kind, b])
            remote(part, part, send_sem.at[kind + 2], recv_sem.at[kind + 2], s, 1 - c).start()
            return carry

        lax.fori_loop(0, GROUP, pass_on, 0)

    pass_all(K, kbuf)
    pass_all(V, vbuf)
    dealt(K, HALF)
    dealt(V, HALF)
    deal_q(1)
    other = pl.ds(pl.multiple_of((1 - c) * HALF, HALF), HALF)
    arrived(kbuf.at[:, other], recv_sem.at[KF])
    arrived(vbuf.at[:, other], recv_sem.at[VF])
    arrived(meta.at[pl.ds(0, GROUP - 1)], meta_sem.at[0])
    arrived(meta.at[pl.ds(0, 3 * GROUP)], meta_sem.at[2])
    arrived(kbuf.at[:, other], send_sem.at[KF])

    scale = jnp.float32(HD**-0.5 * LOG2E)
    ones = jnp.ones((BLK, HD), jnp.bfloat16)

    def attend(u):
        rows = SIZES[u]
        arrived(qbuf[u], recv_sem.at[Q + u])

        def visit(t, carry):
            top, total = carry
            at = jnp.clip(list_s[t, 0], 0, GROUP * GROUP - 1)
            opened = list_s[t, 1] == 1
            key = at % GROUP
            scores = lax.dot_general(
                qbuf[u][at // GROUP], kbuf[key], (((1,), (1,)), ((), ())), preferred_element_type=jnp.float32
            )
            top = jnp.where(opened, -jnp.inf, top)
            new_top = jnp.maximum(top, jnp.max(scores, axis=1, keepdims=True))
            weights = jnp.exp2((scores - new_top) * scale).astype(jnp.bfloat16)
            shrink = jnp.exp2((top - new_top) * scale)
            values = jnp.concatenate([vbuf[key], ones], axis=1)
            total = shrink * total + jnp.dot(weights, values, preferred_element_type=jnp.float32)
            state[t, pl.ds(0, rows)] = total
            return new_top, total

        def finish(n, carry, part):
            b = block_at(n)
            total = state[jnp.clip(list_s[n, 2], 0, TILES - 1), pl.ds(0, rows)]
            obuf[u][b] = (total[:, :HD] / total[:, HD:]).astype(jnp.bfloat16)
            dst = att.at[p, pl.ds(FIRSTS[u], rows)]
            landed = back_sem.at[u, part]

            @pl.when(b == p)
            def _():
                pltpu.make_async_copy(obuf[u].at[b], dst, landed).start()

            @pl.when(b != p)
            def _():
                remote(obuf[u].at[b], dst, send_sem.at[O + u], landed, base + b, c).start()

            return carry

        now = (jnp.full((rows, 1), -jnp.inf, jnp.float32), jnp.zeros((rows, 2 * HD), jnp.float32))
        for first, last, done_first, done_last in STEPS:
            now = lax.fori_loop(first, last, visit, now, unroll=last - first)
            lax.fori_loop(done_first, done_last, functools.partial(finish, part=done_first // 8), 0)

    def project(part):
        for u in range(CHUNKS):
            arrived(att.at[pl.ds(0, 8), pl.ds(0, SIZES[u])], back_sem.at[u, part])
        heads = [
            (y + 4 - (STEP_Y >> 2 * m & 3) + 2 * k) % 4 * 4 + (x + 4 - (STEP_X >> 2 * m & 3)) % 4
            for m in range(4 * part, 4 * part + 4)
            for k in range(2)
        ]
        left = jnp.concatenate([att[h] for h in heads], axis=1)

        def tile(n, carry):
            cols = pl.ds(pl.multiple_of(n * COLS, COLS), COLS)
            right = jnp.concatenate([wbuf[pl.ds(pl.multiple_of(h * HD, HD), HD), cols] for h in heads], axis=0)
            product = jnp.dot(left, right, preferred_element_type=jnp.float32)
            if part == 0:
                partial_sum[:, cols] = product
            else:
                out[:, cols] = (partial_sum[:, cols] + product).astype(jnp.bfloat16)
            return carry

        lax.fori_loop(0, wbuf.shape[1] // COLS, tile, 0, unroll=PROJ_UNROLL)

    for u in range(CHUNKS):
        attend(u)
    w_own.wait()
    w_sent.wait()
    arrived(vbuf.at[:, other], send_sem.at[VF])
    for u in range(CHUNKS):
        dealt(Q + u, SIZES[u])
    project(0)
    project(1)
    for u in range(CHUNKS):
        arrived(obuf[u].at[pl.ds(0, GROUP - 1)], send_sem.at[O + u])


def local(query_states, key_states, value_states, doc_ids, pair_table, out_weight):
    bf16, dma = jnp.bfloat16, pltpu.SemaphoreType.DMA
    anywhere = pl.BlockSpec(memory_space=pl.ANY)
    width = out_weight.shape[1]
    return pl.pallas_call(
        kernel,
        out_shape=pltpu.VMEM((HALF, width), bf16),
        in_specs=[anywhere] * 6,
        out_specs=pl.BlockSpec(memory_space=pltpu.VMEM),
        scratch_shapes=[
            pltpu.VMEM((GROUP, BLK, HD), bf16),
            pltpu.VMEM((GROUP, BLK, HD), bf16),
            pltpu.VMEM((TILES, MOST, 2 * HD), jnp.float32),
            pltpu.VMEM((2048, width), bf16),
            pltpu.VMEM((64, 8, 128), jnp.int32),
            pltpu.VMEM((64, 128), jnp.int32),
            pltpu.SMEM((64, 128), jnp.int32),
            pltpu.SMEM((1,), jnp.int32),
            pltpu.SMEM((2, 3), jnp.int32),
        ]
        + [pltpu.VMEM((GROUP, rows, HD), bf16) for rows in SIZES]
        + [pltpu.VMEM((GROUP, rows, HD), bf16) for rows in SIZES]
        + [pltpu.VMEM((GROUP, HALF, HD), bf16), pltpu.VMEM((HALF, width), jnp.float32)]
        + [dma((KINDS,)), dma((KINDS,)), dma((CHUNKS, 2)), dma((2, GROUP)), dma((4,)), dma((3,)), dma((2,))],
        compiler_params=pltpu.CompilerParams(
            collective_id=0, has_side_effects=True, vmem_limit_bytes=56 << 20
        ),
    )(query_states, key_states, value_states, doc_ids, pair_table.T, out_weight)


def solution(mesh):
    placed = (
        P("seq", "head"),
        P("seq", "head"),
        P("seq", "head"),
        P("seq"),
        P("seq", None),
        P("head", None),
    )
    return jax.shard_map(
        local, mesh=mesh, in_specs=placed, out_specs=P(("seq", "head"), None), check_vma=False
    )
```

```python
import functools

import jax
import jax.numpy as jnp
from jax import lax
from jax.experimental import pallas as pl
from jax.experimental.pallas import tpu as pltpu
from jax.sharding import PartitionSpec as P

HD = 128
BLK = 512
GROUP = 16
HALF = BLK // 2
TILES = 64
SIZES = (128, 128)
FIRSTS = (0, 128)
STEPS = ((0, 24, 0, 4), (24, 48, 4, 8), (48, 64, 8, 16))
PROJ_UNROLL = 8
STEP_X = sum(d << 2 * n for n, d in enumerate((2, 2, 1, 3, 1, 3, 0, 0)))
STEP_Y = sum(d << 2 * n for n, d in enumerate((1, 0, 1, 1, 0, 0, 1, 0)))
CHUNKS = len(SIZES)
MOST = max(SIZES)
COLS = 512
LOG2E = 1.4426950408889634
MESH = pl.DeviceIdType.MESH

K, V, KF, VF, Q, O = 0, 1, 2, 3, 4, 4 + CHUNKS
KINDS = 4 + 2 * CHUNKS


def kernel(
    q_in, k_in, v_in, doc_in, pair_in, w_in, out,
    kbuf, vbuf, state, wbuf, meta, list_v, list_s, doc_s, pair_s, *rest,
):
    qbuf, obuf = rest[:CHUNKS], rest[CHUNKS : 2 * CHUNKS]
    att, partial_sum, send_sem, recv_sem, back_sem, block_sem, meta_sem, w_sem, own_sem = rest[2 * CHUNKS :]
    s, c = lax.axis_index("seq"), lax.axis_index("head")
    plane = s // GROUP
    base = plane * GROUP
    p = s - base

    def remote(src, dst, ssem, rsem, seq, core):
        return pltpu.make_async_remote_copy(
            src_ref=src, dst_ref=dst, send_sem=ssem, recv_sem=rsem,
            device_id=(seq, core), device_id_type=MESH,
        )

    def arrived(ref, sem):
        pltpu.make_async_copy(ref, ref, sem).wait()

    x, y = p % 4, p // 4

    def block_at(place):
        step = place // 2 * 2
        return (y + (STEP_Y >> step & 3) + place % 2 * 2) % 4 * 4 + (x + (STEP_X >> step & 3)) % 4

    barrier = pltpu.get_barrier_semaphore()

    def greet(n, carry):
        pl.semaphore_signal(barrier, inc=1, device_id=(base + (p + n) % GROUP, c), device_id_type=MESH)
        pl.semaphore_signal(barrier, inc=1, device_id=(base + (p + n) % GROUP, 1 - c), device_id_type=MESH)
        return carry

    def greet_far(n, carry):
        pl.semaphore_signal(barrier, inc=1, device_id=((plane + n) % 4 * GROUP + p, c), device_id_type=MESH)
        return carry

    lax.fori_loop(1, GROUP, greet, 0)
    lax.fori_loop(1, 4, greet_far, 0)
    pl.semaphore_signal(barrier, inc=1, device_id=(s, 1 - c), device_id_type=MESH)

    w_rows = pl.ds(pl.multiple_of(c * 1024, 1024), 1024)
    w_own = pltpu.make_async_copy(w_in, wbuf.at[w_rows], w_sem.at[0])
    w_own.start()
    doc_copy = pltpu.make_async_copy(doc_in, doc_s, own_sem.at[0])
    pair_copy = pltpu.make_async_copy(pair_in, pair_s, own_sem.at[1])
    doc_copy.start()
    pair_copy.start()
    doc_copy.wait()
    pair_copy.wait()
    lane = lax.broadcasted_iota(jnp.int32, (8, 128), 1)
    row = jnp.where(lane == 0, doc_s[0], 0)
    for r in range(3):
        row = jnp.where(lane == r + 1, pair_s[0, r] * 64 + pair_s[1, r], row)
    meta[pl.ds(s, 1)] = row[None]
    pl.semaphore_wait(barrier, 2 * GROUP - 1 + 3)

    def meta_copy(n, carry):
        own = meta.at[pl.ds(s, 1)]
        remote(own, own, meta_sem.at[0], meta_sem.at[1], base + (p + n) % GROUP, c).start()
        return carry

    def far_copy(n, carry):
        rows = meta.at[pl.ds(base, GROUP)]
        remote(rows, rows, meta_sem.at[2], meta_sem.at[3], (plane + n) % 4 * GROUP + p, c).start()
        return carry

    lax.fori_loop(1, GROUP, meta_copy, 0)

    def deal(kind, ref, dst, recv, first_row, rows):
        def step(n, carry):
            i = (5 * n + p + 2) % 8
            seq = base + 8 * c + i
            for j in range(2):
                src = ref.at[pl.ds(j * HALF + first_row, rows), pl.ds(pl.multiple_of(i * HD, HD), HD)]
                mine = (seq == s) & (c == j)

                @pl.when(mine)
                def _(src=src, j=j):
                    pltpu.make_async_copy(src, dst(j), recv).start()

                @pl.when(jnp.logical_not(mine))
                def _(src=src, j=j):
                    remote(src, dst(j), send_sem.at[kind], recv, seq, j).start()

            return carry

        lax.fori_loop(0, 8, step, 0)

    def dealt(kind, rows):
        own = p // 8 == c

        @pl.when(own)
        def _():
            arrived(kbuf.at[pl.ds(0, GROUP - 1), pl.ds(0, rows)], send_sem.at[kind])

        @pl.when(jnp.logical_not(own))
        def _():
            arrived(kbuf.at[:, pl.ds(0, rows)], send_sem.at[kind])

    def half_of(buf, b, j):
        return buf.at[b, pl.ds(pl.multiple_of(j * HALF, HALF), HALF)]

    def deal_q(u):
        deal(Q + u, q_in, lambda j: qbuf[u].at[p], recv_sem.at[Q + u], FIRSTS[u], SIZES[u])

    deal(K, k_in, lambda j: half_of(kbuf, p, j), block_sem.at[K, p], 0, HALF)
    deal(V, v_in, lambda j: half_of(vbuf, p, j), block_sem.at[V, p], 0, HALF)
    w_sent = remote(w_in, wbuf.at[w_rows], w_sem.at[1], w_sem.at[2], s, 1 - c)
    w_sent.start()
    deal_q(0)
    deal_q(1)

    arrived(meta.at[pl.ds(0, GROUP - 1)], meta_sem.at[1])
    lax.fori_loop(1, 4, far_copy, 0)
    arrived(meta.at[pl.ds(0, 3 * GROUP)], meta_sem.at[3])

    table = meta[:, 0, :]
    cell = lax.broadcasted_iota(jnp.int32, (64, 256), 1)
    place = lax.broadcasted_iota(jnp.int32, (64, 256), 0)
    qb = block_at(cell // GROUP)
    qa, ka = qb + base, cell % GROUP + base
    code = jnp.minimum(qa, ka) * 64 + jnp.maximum(qa, ka)
    hit = (code == table[:, 1:2]) | (code == table[:, 2:3]) | (code == table[:, 3:4])
    listed = jnp.max(jnp.where(hit, 1.0, 0.0), axis=0, keepdims=True)
    docs = table[:, 0:1]
    doc_q = jnp.sum(jnp.where(place == qa, docs, 0).astype(jnp.float32), axis=0, keepdims=True)
    doc_k = jnp.sum(jnp.where(place == ka, docs, 0).astype(jnp.float32), axis=0, keepdims=True)
    alive = jnp.where((qa[:1] == ka[:1]) | ((listed > 0.5) & (doc_q == doc_k)), 1.0, 0.0)
    upto = jnp.where(
        lax.broadcasted_iota(jnp.int32, (256, 256), 0) <= lax.broadcasted_iota(jnp.int32, (256, 256), 1), 1.0, 0.0
    )
    rank = jnp.dot(
        jnp.broadcast_to(alive, (16, 256)).astype(jnp.bfloat16), upto.astype(jnp.bfloat16),
        preferred_element_type=jnp.float32,
    )[:1]
    pick = jnp.where((alive > 0.5) & (rank == (place + 1).astype(jnp.float32)), 1.0, 0.0)
    cells = jnp.sum(pick * (qb * GROUP + cell % GROUP).astype(jnp.float32), axis=1, keepdims=True)
    rank_64 = jnp.broadcast_to(rank, (64, 256))
    ends = jnp.sum(jnp.where(cell == place * GROUP + GROUP - 1, rank_64 - 1.0, 0.0), axis=1, keepdims=True)
    opens = jnp.max(
        jnp.where((cell % GROUP == GROUP - 1) & (rank_64 == place.astype(jnp.float32)), 1.0, 0.0), axis=1, keepdims=True
    )
    wide = lax.broadcasted_iota(jnp.int32, (64, 128), 1)
    table_out = jnp.where(wide == 0, cells, jnp.where(wide == 1, opens, jnp.where(wide == 2, ends, 0.0)))
    list_v[...] = table_out.astype(jnp.int32)
    to_scalar = pltpu.make_async_copy(list_v, list_s, own_sem.at[0])
    to_scalar.start()
    to_scalar.wait()

    def pass_all(kind, buf):
        def pass_on(n, carry):
            b = (p + n) % GROUP
            part = half_of(buf, b, c)
            arrived(part, block_sem.at[kind, b])
            remote(part, part, send_sem.at[kind + 2], recv_sem.at[kind + 2], s, 1 - c).start()
            return carry

        lax.fori_loop(0, GROUP, pass_on, 0)

    pass_all(K, kbuf)
    pass_all(V, vbuf)
    dealt(K, HALF)
    dealt(V, HALF)
    other = pl.ds(pl.multiple_of((1 - c) * HALF, HALF), HALF)
    arrived(kbuf.at[:, other], recv_sem.at[KF])
    arrived(vbuf.at[:, other], recv_sem.at[VF])
    arrived(meta.at[pl.ds(0, GROUP - 1)], meta_sem.at[0])
    arrived(meta.at[pl.ds(0, 3 * GROUP)], meta_sem.at[2])
    arrived(kbuf.at[:, other], send_sem.at[KF])

    scale = jnp.float32(HD**-0.5 * LOG2E)
    ones = jnp.ones((BLK, HD), jnp.bfloat16)

    def attend(u):
        rows = SIZES[u]
        arrived(qbuf[u], recv_sem.at[Q + u])

        def visit(t, carry):
            top, total = carry
            at = jnp.clip(list_s[t, 0], 0, GROUP * GROUP - 1)
            opened = list_s[t, 1] == 1
            key = at % GROUP
            scores = lax.dot_general(
                qbuf[u][at // GROUP], kbuf[key], (((1,), (1,)), ((), ())), preferred_element_type=jnp.float32
            )
            top = jnp.where(opened, -jnp.inf, top)
            new_top = jnp.maximum(top, jnp.max(scores, axis=1, keepdims=True))
            weights = jnp.exp2((scores - new_top) * scale).astype(jnp.bfloat16)
            shrink = jnp.exp2((top - new_top) * scale)
            values = jnp.concatenate([vbuf[key], ones], axis=1)
            total = shrink * total + jnp.dot(weights, values, preferred_element_type=jnp.float32)
            state[t, pl.ds(0, rows)] = total
            return new_top, total

        def finish(n, carry, part):
            b = block_at(n)
            total = state[jnp.clip(list_s[n, 2], 0, TILES - 1), pl.ds(0, rows)]
            obuf[u][b] = (total[:, :HD] / total[:, HD:]).astype(jnp.bfloat16)
            dst = att.at[p, pl.ds(FIRSTS[u], rows)]
            landed = back_sem.at[u, part]

            @pl.when(b == p)
            def _():
                pltpu.make_async_copy(obuf[u].at[b], dst, landed).start()

            @pl.when(b != p)
            def _():
                remote(obuf[u].at[b], dst, send_sem.at[O + u], landed, base + b, c).start()

            return carry

        now = (jnp.full((rows, 1), -jnp.inf, jnp.float32), jnp.zeros((rows, 2 * HD), jnp.float32))
        for first, last, done_first, done_last in STEPS:
            now = lax.fori_loop(first, last, visit, now, unroll=last - first)
            lax.fori_loop(done_first, done_last, functools.partial(finish, part=done_first // 8), 0)

    def project(part):
        for u in range(CHUNKS):
            arrived(att.at[pl.ds(0, 8), pl.ds(0, SIZES[u])], back_sem.at[u, part])
        heads = [
            (y + 4 - (STEP_Y >> 2 * m & 3) + 2 * k) % 4 * 4 + (x + 4 - (STEP_X >> 2 * m & 3)) % 4
            for m in range(4 * part, 4 * part + 4)
            for k in range(2)
        ]
        left = jnp.concatenate([att[h] for h in heads], axis=1)

        def tile(n, carry):
            cols = pl.ds(pl.multiple_of(n * COLS, COLS), COLS)
            right = jnp.concatenate([wbuf[pl.ds(pl.multiple_of(h * HD, HD), HD), cols] for h in heads], axis=0)
            product = jnp.dot(left, right, preferred_element_type=jnp.float32)
            if part == 0:
                partial_sum[:, cols] = product
            else:
                out[:, cols] = (partial_sum[:, cols] + product).astype(jnp.bfloat16)
            return carry

        lax.fori_loop(0, wbuf.shape[1] // COLS, tile, 0, unroll=PROJ_UNROLL)

    for u in range(CHUNKS):
        attend(u)
    w_own.wait()
    w_sent.wait()
    arrived(vbuf.at[:, other], send_sem.at[VF])
    for u in range(CHUNKS):
        dealt(Q + u, SIZES[u])
    project(0)
    project(1)
    for u in range(CHUNKS):
        arrived(obuf[u].at[pl.ds(0, GROUP - 1)], send_sem.at[O + u])


def local(query_states, key_states, value_states, doc_ids, pair_table, out_weight):
    bf16, dma = jnp.bfloat16, pltpu.SemaphoreType.DMA
    anywhere = pl.BlockSpec(memory_space=pl.ANY)
    width = out_weight.shape[1]
    return pl.pallas_call(
        kernel,
        out_shape=pltpu.VMEM((HALF, width), bf16),
        in_specs=[anywhere] * 6,
        out_specs=pl.BlockSpec(memory_space=pltpu.VMEM),
        scratch_shapes=[
            pltpu.VMEM((GROUP, BLK, HD), bf16),
            pltpu.VMEM((GROUP, BLK, HD), bf16),
            pltpu.VMEM((TILES, MOST, 2 * HD), jnp.float32),
            pltpu.VMEM((2048, width), bf16),
            pltpu.VMEM((64, 8, 128), jnp.int32),
            pltpu.VMEM((64, 128), jnp.int32),
            pltpu.SMEM((64, 128), jnp.int32),
            pltpu.SMEM((1,), jnp.int32),
            pltpu.SMEM((2, 3), jnp.int32),
        ]
        + [pltpu.VMEM((GROUP, rows, HD), bf16) for rows in SIZES]
        + [pltpu.VMEM((GROUP, rows, HD), bf16) for rows in SIZES]
        + [pltpu.VMEM((GROUP, HALF, HD), bf16), pltpu.VMEM((HALF, width), jnp.float32)]
        + [dma((KINDS,)), dma((KINDS,)), dma((CHUNKS, 2)), dma((2, GROUP)), dma((4,)), dma((3,)), dma((2,))],
        compiler_params=pltpu.CompilerParams(
            collective_id=0, has_side_effects=True, vmem_limit_bytes=56 << 20
        ),
    )(query_states, key_states, value_states, doc_ids, pair_table.T, out_weight)


def solution(mesh):
    placed = (
        P("seq", "head"),
        P("seq", "head"),
        P("seq", "head"),
        P("seq"),
        P("seq", None),
        P("head", None),
    )
    return jax.shard_map(
        local, mesh=mesh, in_specs=placed, out_specs=P(("seq", "head"), None), check_vma=False
    )
```

```python
import functools

import jax
import jax.numpy as jnp
from jax import lax
from jax.experimental import pallas as pl
from jax.experimental.pallas import tpu as pltpu
from jax.sharding import PartitionSpec as P

HD = 128
BLK = 512
GROUP = 16
HALF = BLK // 2
TILES = 64
SIZES = (128, 128)
FIRSTS = (0, 128)
STEPS = ((0, 24, 0, 4), (24, 48, 4, 8), (48, 64, 8, 16))
PROJ_UNROLL = 8
STEP_X = sum(d << 2 * n for n, d in enumerate((2, 2, 1, 3, 1, 3, 0, 0)))
STEP_Y = sum(d << 2 * n for n, d in enumerate((1, 0, 1, 1, 0, 0, 1, 0)))
CHUNKS = len(SIZES)
MOST = max(SIZES)
COLS = 512
LOG2E = 1.4426950408889634
MESH = pl.DeviceIdType.MESH

K, V, KF, VF, Q, O = 0, 1, 2, 3, 4, 4 + CHUNKS
KINDS = 4 + 2 * CHUNKS


def kernel(
    q_in, k_in, v_in, doc_in, pair_in, w_in, out,
    kbuf, vbuf, state, wbuf, meta, list_v, list_s, doc_s, pair_s, *rest,
):
    qbuf, obuf = rest[:CHUNKS], rest[CHUNKS : 2 * CHUNKS]
    att, partial_sum, send_sem, recv_sem, back_sem, block_sem, meta_sem, w_sem, own_sem = rest[2 * CHUNKS :]
    s, c = lax.axis_index("seq"), lax.axis_index("head")
    plane = s // GROUP
    base = plane * GROUP
    p = s - base

    def remote(src, dst, ssem, rsem, seq, core):
        return pltpu.make_async_remote_copy(
            src_ref=src, dst_ref=dst, send_sem=ssem, recv_sem=rsem,
            device_id=(seq, core), device_id_type=MESH,
        )

    def arrived(ref, sem):
        pltpu.make_async_copy(ref, ref, sem).wait()

    x, y = p % 4, p // 4

    def block_at(place):
        step = place // 2 * 2
        return (y + (STEP_Y >> step & 3) + place % 2 * 2) % 4 * 4 + (x + (STEP_X >> step & 3)) % 4

    barrier = pltpu.get_barrier_semaphore()

    def greet(n, carry):
        pl.semaphore_signal(barrier, inc=1, device_id=(base + (p + n) % GROUP, c), device_id_type=MESH)
        pl.semaphore_signal(barrier, inc=1, device_id=(base + (p + n) % GROUP, 1 - c), device_id_type=MESH)
        return carry

    def greet_far(n, carry):
        pl.semaphore_signal(barrier, inc=1, device_id=((plane + n) % 4 * GROUP + p, c), device_id_type=MESH)
        return carry

    lax.fori_loop(1, GROUP, greet, 0)
    lax.fori_loop(1, 4, greet_far, 0)
    pl.semaphore_signal(barrier, inc=1, device_id=(s, 1 - c), device_id_type=MESH)

    w_rows = pl.ds(pl.multiple_of(c * 1024, 1024), 1024)
    w_own = pltpu.make_async_copy(w_in, wbuf.at[w_rows], w_sem.at[0])
    w_own.start()
    doc_copy = pltpu.make_async_copy(doc_in, doc_s, own_sem.at[0])
    pair_copy = pltpu.make_async_copy(pair_in, pair_s, own_sem.at[1])
    doc_copy.start()
    pair_copy.start()
    doc_copy.wait()
    pair_copy.wait()
    lane = lax.broadcasted_iota(jnp.int32, (8, 128), 1)
    row = jnp.where(lane == 0, doc_s[0], 0)
    for r in range(3):
        row = jnp.where(lane == r + 1, pair_s[0, r] * 64 + pair_s[1, r], row)
    meta[pl.ds(s, 1)] = row[None]
    pl.semaphore_wait(barrier, 2 * GROUP - 1 + 3)

    def meta_copy(n, carry):
        own = meta.at[pl.ds(s, 1)]
        remote(own, own, meta_sem.at[0], meta_sem.at[1], base + (p + n) % GROUP, c).start()
        return carry

    def far_copy(n, carry):
        rows = meta.at[pl.ds(base, GROUP)]
        remote(rows, rows, meta_sem.at[2], meta_sem.at[3], (plane + n) % 4 * GROUP + p, c).start()
        return carry

    lax.fori_loop(1, GROUP, meta_copy, 0)

    def deal(kind, ref, dst, recv, first_row, rows):
        def step(n, carry):
            i = (5 * n + p + 2) % 8
            seq = base + 8 * c + i
            for j in range(2):
                src = ref.at[pl.ds(j * HALF + first_row, rows), pl.ds(pl.multiple_of(i * HD, HD), HD)]
                mine = (seq == s) & (c == j)

                @pl.when(mine)
                def _(src=src, j=j):
                    pltpu.make_async_copy(src, dst(j), recv).start()

                @pl.when(jnp.logical_not(mine))
                def _(src=src, j=j):
                    remote(src, dst(j), send_sem.at[kind], recv, seq, j).start()

            return carry

        lax.fori_loop(0, 8, step, 0)

    def dealt(kind, rows):
        own = p // 8 == c

        @pl.when(own)
        def _():
            arrived(kbuf.at[pl.ds(0, GROUP - 1), pl.ds(0, rows)], send_sem.at[kind])

        @pl.when(jnp.logical_not(own))
        def _():
            arrived(kbuf.at[:, pl.ds(0, rows)], send_sem.at[kind])

    def half_of(buf, b, j):
        return buf.at[b, pl.ds(pl.multiple_of(j * HALF, HALF), HALF)]

    def deal_q(u):
        deal(Q + u, q_in, lambda j: qbuf[u].at[p], recv_sem.at[Q + u], FIRSTS[u], SIZES[u])

    deal(K, k_in, lambda j: half_of(kbuf, p, j), block_sem.at[K, p], 0, HALF)
    deal(V, v_in, lambda j: half_of(vbuf, p, j), block_sem.at[V, p], 0, HALF)
    w_sent = remote(w_in, wbuf.at[w_rows], w_sem.at[1], w_sem.at[2], s, 1 - c)
    w_sent.start()
    deal_q(0)
    deal_q(1)

    arrived(meta.at[pl.ds(0, GROUP - 1)], meta_sem.at[1])
    lax.fori_loop(1, 4, far_copy, 0)
    arrived(meta.at[pl.ds(0, 3 * GROUP)], meta_sem.at[3])

    table = meta[:, 0, :]
    cell = lax.broadcasted_iota(jnp.int32, (64, 256), 1)
    place = lax.broadcasted_iota(jnp.int32, (64, 256), 0)
    qb = block_at(cell // GROUP)
    qa, ka = qb + base, cell % GROUP + base
    code = jnp.minimum(qa, ka) * 64 + jnp.maximum(qa, ka)
    hit = (code == table[:, 1:2]) | (code == table[:, 2:3]) | (code == table[:, 3:4])
    listed = jnp.max(jnp.where(hit, 1.0, 0.0), axis=0, keepdims=True)
    docs = table[:, 0:1]
    doc_q = jnp.sum(jnp.where(place == qa, docs, 0).astype(jnp.float32), axis=0, keepdims=True)
    doc_k = jnp.sum(jnp.where(place == ka, docs, 0).astype(jnp.float32), axis=0, keepdims=True)
    alive = jnp.where((qa[:1] == ka[:1]) | ((listed > 0.5) & (doc_q == doc_k)), 1.0, 0.0)
    upto = jnp.where(
        lax.broadcasted_iota(jnp.int32, (256, 256), 0) <= lax.broadcasted_iota(jnp.int32, (256, 256), 1), 1.0, 0.0
    )
    rank = jnp.dot(
        jnp.broadcast_to(alive, (16, 256)).astype(jnp.bfloat16), upto.astype(jnp.bfloat16),
        preferred_element_type=jnp.float32,
    )[:1]
    pick = jnp.where((alive > 0.5) & (rank == (place + 1).astype(jnp.float32)), 1.0, 0.0)
    cells = jnp.sum(pick * (qb * GROUP + cell % GROUP).astype(jnp.float32), axis=1, keepdims=True)
    rank_64 = jnp.broadcast_to(rank, (64, 256))
    ends = jnp.sum(jnp.where(cell == place * GROUP + GROUP - 1, rank_64 - 1.0, 0.0), axis=1, keepdims=True)
    opens = jnp.max(
        jnp.where((cell % GROUP == GROUP - 1) & (rank_64 == place.astype(jnp.float32)), 1.0, 0.0), axis=1, keepdims=True
    )
    wide = lax.broadcasted_iota(jnp.int32, (64, 128), 1)
    table_out = jnp.where(wide == 0, cells, jnp.where(wide == 1, opens, jnp.where(wide == 2, ends, 0.0)))
    list_v[...] = table_out.astype(jnp.int32)
    to_scalar = pltpu.make_async_copy(list_v, list_s, own_sem.at[0])
    to_scalar.start()
    to_scalar.wait()

    def pass_all(kind, buf):
        def pass_on(n, carry):
            b = (p + n) % GROUP
            part = half_of(buf, b, c)
            arrived(part, block_sem.at[kind, b])
            remote(part, part, send_sem.at[kind + 2], recv_sem.at[kind + 2], s, 1 - c).start()
            return carry

        lax.fori_loop(0, GROUP, pass_on, 0)

    pass_all(K, kbuf)
    pass_all(V, vbuf)
    dealt(K, HALF)
    dealt(V, HALF)
    other = pl.ds(pl.multiple_of((1 - c) * HALF, HALF), HALF)
    arrived(kbuf.at[:, other], recv_sem.at[KF])
    arrived(vbuf.at[:, other], recv_sem.at[VF])
    arrived(meta.at[pl.ds(0, GROUP - 1)], meta_sem.at[0])
    arrived(meta.at[pl.ds(0, 3 * GROUP)], meta_sem.at[2])
    arrived(kbuf.at[:, other], send_sem.at[KF])

    scale = jnp.float32(HD**-0.5 * LOG2E)
    ones = jnp.ones((BLK, HD), jnp.bfloat16)

    def attend(u):
        rows = SIZES[u]
        arrived(qbuf[u], recv_sem.at[Q + u])

        def visit(t, carry):
            top, total = carry
            at = jnp.clip(list_s[t, 0], 0, GROUP * GROUP - 1)
            opened = list_s[t, 1] == 1
            key = at % GROUP
            scores = lax.dot_general(
                qbuf[u][at // GROUP], kbuf[key], (((1,), (1,)), ((), ())), preferred_element_type=jnp.float32
            )
            top = jnp.where(opened, -jnp.inf, top)
            new_top = jnp.maximum(top, jnp.max(scores, axis=1, keepdims=True))
            weights = jnp.exp2((scores - new_top) * scale).astype(jnp.bfloat16)
            shrink = jnp.exp2((top - new_top) * scale)
            values = jnp.concatenate([vbuf[key], ones], axis=1)
            total = shrink * total + jnp.dot(weights, values, preferred_element_type=jnp.float32)
            state[t, pl.ds(0, rows)] = total
            return new_top, total

        def finish(n, carry):
            b = block_at(n)
            total = state[jnp.clip(list_s[n, 2], 0, TILES - 1), pl.ds(0, rows)]
            obuf[u][b] = (total[:, :HD] / total[:, HD:]).astype(jnp.bfloat16)
            return carry

        def send(n, carry, part):
            b = block_at(n)
            dst = att.at[p, pl.ds(FIRSTS[u], rows)]
            landed = back_sem.at[u, part]

            @pl.when(b == p)
            def _():
                pltpu.make_async_copy(obuf[u].at[b], dst, landed).start()

            @pl.when(b != p)
            def _():
                remote(obuf[u].at[b], dst, send_sem.at[O + u], landed, base + b, c).start()

            return carry

        now = (jnp.full((rows, 1), -jnp.inf, jnp.float32), jnp.zeros((rows, 2 * HD), jnp.float32))
        for first, last, done_first, done_last in STEPS:
            now = lax.fori_loop(first, last, visit, now, unroll=last - first)
            lax.fori_loop(done_first, done_last, finish, 0, unroll=4)
            lax.fori_loop(done_first, done_last, functools.partial(send, part=done_first // 8), 0)

    def project(part):
        for u in range(CHUNKS):
            arrived(att.at[pl.ds(0, 8), pl.ds(0, SIZES[u])], back_sem.at[u, part])
        heads = [
            (y + 4 - (STEP_Y >> 2 * m & 3) + 2 * k) % 4 * 4 + (x + 4 - (STEP_X >> 2 * m & 3)) % 4
            for m in range(4 * part, 4 * part + 4)
            for k in range(2)
        ]
        left = jnp.concatenate([att[h] for h in heads], axis=1)

        def tile(n, carry):
            cols = pl.ds(pl.multiple_of(n * COLS, COLS), COLS)
            right = jnp.concatenate([wbuf[pl.ds(pl.multiple_of(h * HD, HD), HD), cols] for h in heads], axis=0)
            product = jnp.dot(left, right, preferred_element_type=jnp.float32)
            if part == 0:
                partial_sum[:, cols] = product
            else:
                out[:, cols] = (partial_sum[:, cols] + product).astype(jnp.bfloat16)
            return carry

        lax.fori_loop(0, wbuf.shape[1] // COLS, tile, 0, unroll=PROJ_UNROLL)

    for u in range(CHUNKS):
        attend(u)
    w_own.wait()
    w_sent.wait()
    arrived(vbuf.at[:, other], send_sem.at[VF])
    for u in range(CHUNKS):
        dealt(Q + u, SIZES[u])
    project(0)
    project(1)
    for u in range(CHUNKS):
        arrived(obuf[u].at[pl.ds(0, GROUP - 1)], send_sem.at[O + u])


def local(query_states, key_states, value_states, doc_ids, pair_table, out_weight):
    bf16, dma = jnp.bfloat16, pltpu.SemaphoreType.DMA
    anywhere = pl.BlockSpec(memory_space=pl.ANY)
    width = out_weight.shape[1]
    return pl.pallas_call(
        kernel,
        out_shape=pltpu.VMEM((HALF, width), bf16),
        in_specs=[anywhere] * 6,
        out_specs=pl.BlockSpec(memory_space=pltpu.VMEM),
        scratch_shapes=[
            pltpu.VMEM((GROUP, BLK, HD), bf16),
            pltpu.VMEM((GROUP, BLK, HD), bf16),
            pltpu.VMEM((TILES, MOST, 2 * HD), jnp.float32),
            pltpu.VMEM((2048, width), bf16),
            pltpu.VMEM((64, 8, 128), jnp.int32),
            pltpu.VMEM((64, 128), jnp.int32),
            pltpu.SMEM((64, 128), jnp.int32),
            pltpu.SMEM((1,), jnp.int32),
            pltpu.SMEM((2, 3), jnp.int32),
        ]
        + [pltpu.VMEM((GROUP, rows, HD), bf16) for rows in SIZES]
        + [pltpu.VMEM((GROUP, rows, HD), bf16) for rows in SIZES]
        + [pltpu.VMEM((GROUP, HALF, HD), bf16), pltpu.VMEM((HALF, width), jnp.float32)]
        + [dma((KINDS,)), dma((KINDS,)), dma((CHUNKS, 2)), dma((2, GROUP)), dma((4,)), dma((3,)), dma((2,))],
        compiler_params=pltpu.CompilerParams(
            collective_id=0, has_side_effects=True, vmem_limit_bytes=56 << 20
        ),
    )(query_states, key_states, value_states, doc_ids, pair_table.T, out_weight)


def solution(mesh):
    placed = (
        P("seq", "head"),
        P("seq", "head"),
        P("seq", "head"),
        P("seq"),
        P("seq", None),
        P("head", None),
    )
    return jax.shard_map(
        local, mesh=mesh, in_specs=placed, out_specs=P(("seq", "head"), None), check_vma=False
    )
```
